256 devices in a mesh: dp: 8 (over z), ctx: 32 (over x, y, core).
Axes of the slice: x: 4, y: 4, z: 8, core: 2. Of those that a mesh axis runs over, the one named last changes fastest.
Arguments:
- query_rows: bfloat16 [131072, 1024], P(('dp', 'ctx')), parts along dimension 0, may hold values from -6 to 6
- key_rows: bfloat16 [131072, 1024], P(('dp', 'ctx')), parts along dimension 0, may hold values from -6 to 6
- value_rows: bfloat16 [131072, 1024], P(('dp', 'ctx')), parts along dimension 0, may hold values from -6 to 6
- summary_pos: int32 [64, 16], P('dp'), parts along dimension 0, may hold values from 0 to 2047, as said below
Outputs:
- attended: bfloat16 [131072, 1024], P(('dp', 'ctx')), parts along dimension 0
The draws below stay inside these ranges and needn't reach their ends.
There are 8 independent parts, one for each index of `dp`. The reference program is written for one: setup_inputs(seed, part) draws one part's arguments, and reference() takes and returns one part's arrays. A program takes and returns all parts, laid end to end along the dimension named above; each array names one. Nothing has to cross between parts.
Inputs may be any that keep to these rules, and one draw needn't show every extreme that they name: `summary_pos`: each row holds 16 distinct offsets.
All inputs are finite; a program needn't handle non-finite values.
Results may differ from the reference program's by a relative error of at most 0.003.
Values may be sent and summed in bfloat16 or wider, within the bound.
A program may use at most 192 MiB of HBM per device.

```python
import jax
import jax.numpy as jnp
from jax import lax

H = 8
HD = 128
D = 1024
STRIDE = 2048
SUMS = 16
TOK_DEV = 512
TOKENS = 16384


def summary_offsets(key):
    row_keys = jax.random.split(jax.random.fold_in(key, 5), TOKENS // STRIDE)

    def one_row(row_key):
        return jax.random.permutation(row_key, STRIDE)[:SUMS]
    return jax.vmap(one_row)(row_keys).astype(jnp.int32)


def draw_summary_pos(key, part):
    return summary_offsets(key)


def drawn_field(key, salt_value):
    return jnp.clip(1.5 * jax.random.normal(jax.random.fold_in(key, salt_value), (TOKENS, D), jnp.float32), -6.0, 6.0)


def draw_query_rows(key, part):
    field = drawn_field(key, 1)
    return field.astype(jnp.bfloat16)


def draw_key_rows(key, part):
    field = drawn_field(key, 2)
    return field.astype(jnp.bfloat16)


def levels(key, shape, shards, least, largest):
    loudness = 1.0
    for position, parts in shards:
        draws = jax.random.uniform(jax.random.fold_in(jax.random.fold_in(key, 6), position), (parts,), jnp.float32, least / len(shards), largest / len(shards))
        loudness = loudness * jnp.repeat(jnp.exp(draws), shape[position] // parts).reshape((-1,) + (1,) * (len(shape) - 1 - position))
    return loudness


def normal_values(key, extent, scale, reach, pieces=(), held_as=jnp.bfloat16):
    values = jax.random.normal(key, extent, jnp.float32) * scale
    if len(pieces) > 0:
        values = levels(key, extent, pieces, -0.22, 0.18) * values
    return jnp.clip(values, min=-reach, max=reach).astype(held_as)


def setup_inputs(seed: int = 0, part: int = 0) -> dict:
    arg_keys = jax.random.split(jax.random.key(seed), 5)
    part_splits = jax.random.split(jax.random.fold_in(arg_keys[4], part), 5)
    return {
        "query_rows": draw_query_rows(jax.random.fold_in(jax.random.fold_in(arg_keys[4], part), 71), part),
        "key_rows": draw_key_rows(jax.random.fold_in(jax.random.fold_in(arg_keys[4], part), 71), part),
        "value_rows": normal_values(part_splits[2], (TOKENS, D), 1.0, 6.0, ((0, 32),)),
        "summary_pos": draw_summary_pos(jax.random.fold_in(jax.random.fold_in(arg_keys[4], part), 71), part),
    }


neg_floor = -1.0e30


def group_terms(scores, allowed, value_head):
    masked = jnp.where(allowed, scores, -jnp.inf)
    row_max = jnp.maximum(jnp.max(masked, axis=1), neg_floor)
    weights = jnp.exp(masked - row_max[:, None])
    weight_sum = jnp.sum(weights, axis=1)
    summed = jnp.dot(weights.astype(jnp.bfloat16), value_head, preferred_element_type=jnp.float32)
    return summed, weight_sum, row_max


def merge_groups(partials):
    row_max = partials[0][2]
    for partial_value in partials[1:]:
        row_max = jnp.maximum(row_max, partial_value[2])
    numerator = jnp.zeros_like(partials[0][0])
    denominator = jnp.zeros_like(row_max)
    for summed, weight_sum, group_max in partials:
        factor = jnp.exp(group_max - row_max)
        numerator = numerator + factor[:, None] * summed
        denominator = denominator + factor * weight_sum
    return (numerator / denominator[:, None]).astype(jnp.bfloat16)


def reference(query_rows, key_rows, value_rows, summary_pos):
    stride_count = TOKENS // STRIDE
    shard_count = STRIDE // TOK_DEV
    score_scale = HD ** -0.5
    stride_base = (jnp.arange(stride_count, dtype=jnp.int32) * STRIDE)[:, None]
    row_ids = (stride_base + summary_pos).reshape(-1).astype(jnp.int32)
    summary_keys = key_rows[row_ids]
    summary_values = value_rows[row_ids]
    owner_stride = jnp.repeat(jnp.arange(stride_count, dtype=jnp.int32), SUMS)
    local_rows = jnp.arange(STRIDE, dtype=jnp.int32)
    causal = local_rows[None, :] <= local_rows[:, None]

    def one_stride(stride_index):
        row_start = (stride_index * STRIDE).astype(jnp.int32)
        queries = lax.dynamic_slice_in_dim(query_rows, row_start, STRIDE, 0)
        stride_keys = lax.dynamic_slice_in_dim(key_rows, row_start, STRIDE, 0)
        stride_values = lax.dynamic_slice_in_dim(value_rows, row_start, STRIDE, 0)
        visible = (owner_stride < stride_index)[None, :]

        def one_head(head_index):
            column = (head_index * HD).astype(jnp.int32)
            query_head = lax.dynamic_slice_in_dim(queries, column, HD, 1)
            key_head = lax.dynamic_slice_in_dim(stride_keys, column, HD, 1)
            value_head = lax.dynamic_slice_in_dim(stride_values, column, HD, 1)
            summary_key_head = lax.dynamic_slice_in_dim(summary_keys, column, HD, 1)
            summary_value_head = lax.dynamic_slice_in_dim(summary_values, column, HD, 1)
            summary_scores = jnp.dot(query_head, summary_key_head.T, preferred_element_type=jnp.float32) * score_scale
            band_scores = jnp.dot(query_head, key_head.T, preferred_element_type=jnp.float32) * score_scale
            partials = [group_terms(summary_scores, visible, summary_value_head)]
            for shard_index in range(shard_count):
                shard_low = shard_index * TOK_DEV
                shard_high = shard_low + TOK_DEV
                partials.append(group_terms(band_scores[:, shard_low:shard_high], causal[:, shard_low:shard_high], value_head[shard_low:shard_high]))
            return merge_groups(partials)

        per_head = lax.map(one_head, jnp.arange(H, dtype=jnp.int32))
        return jnp.transpose(per_head, (1, 0, 2)).reshape(STRIDE, H * HD)

    attended = lax.map(one_stride, jnp.arange(stride_count, dtype=jnp.int32))
    return attended.reshape(TOKENS, H * HD)
```

```python
import functools

import jax
import jax.numpy as jnp
import numpy as np
from jax import lax
from jax.experimental import pallas as pl
from jax.experimental.pallas import tpu as pltpu
from jax.sharding import PartitionSpec as P

MESH = pl.DeviceIdType.MESH
HEADS = 8
HD = 128
ROWS = 512
SUMS = 16
STRIDES = 8
X = 4
RATE = float(HD**-0.5 * np.log2(np.e))
FLOOR = -1.0e30


def scores(keys, queries):
    return lax.dot_general(
        keys, queries, (((1,), (1,)), ((), ())), preferred_element_type=jnp.float32
    )


def attend(parts, queries):
    raw = []
    for keys, _, mask in parts:
        s = scores(keys, queries)
        raw.append(s if mask is None else jnp.where(mask, s, FLOOR))
    top = functools.reduce(jnp.maximum, [jnp.max(s, axis=0, keepdims=True) for s in raw]) * RATE
    total = None
    weight = None
    for s, (_, values, _) in zip(raw, parts):
        p = jnp.exp2(s * RATE - top)
        part_weight = jnp.sum(p, axis=0, keepdims=True)
        part = jnp.dot(values, p.astype(jnp.bfloat16), preferred_element_type=jnp.float32)
        total = part if total is None else total + part
        weight = part_weight if weight is None else weight + part_weight
    return total, top, weight


def kernel(
    q_hbm, k_hbm, v_hbm, pos_ref, out_hbm,
    q, k, v, kx, vt, vtx, qr, o_send, o_recv, lse_send, lse_recv,
    acc, acc_max, acc_sum, staged, own_rows, half_recv, half, pair_recv, table,
    load_sem, q_s, q_r, kx_s, kx_r, vt_s, vt_r, o_s, o_r, l_s, l_r, out_sem, st_s, st_r, x_s, x_r,
):
    me = lax.axis_index("ctx")
    core = me % 2
    y = (me // 2) % 4
    x = me // 8
    first = y % 2 == 0
    place = me % 4
    group = y // 2
    stride = x * 2 + group
    peer = me + 1 - 2 * core
    partner = jnp.where(first, me + 2, me - 2)
    beside = x * 8 + (jnp.where(first, y + 3, y + 1) % 4) * 2 + core
    along = [((x + d) % X) * 8 + y * 2 + core for d in range(1, X)]

    loads = [
        pltpu.make_async_copy(src, dst, load_sem.at[n])
        for n, (src, dst) in enumerate(((k_hbm, k), (v_hbm, v), (q_hbm, q)))
    ]
    for load in loads:
        load.start()

    barrier = pltpu.get_barrier_semaphore()
    for other in (peer, partner, beside, *along):
        pl.semaphore_signal(barrier, inc=1, device_id={"ctx": other}, device_id_type=MESH)
    pl.semaphore_wait(barrier, 6)

    def cols(h):
        return pl.ds(pl.multiple_of(h * HD, HD), HD)

    def remote(src, dst, s, r, to):
        return pltpu.make_async_remote_copy(
            src_ref=src, dst_ref=dst, send_sem=s, recv_sem=r, device_id={"ctx": to}, device_id_type=MESH
        )

    def q_copy(h):
        return remote(q_hbm.at[:, cols(h)], qr.at[h], q_s.at[h], q_r.at[h], partner)

    def o_copy(h):
        return remote(o_send.at[h], o_recv.at[h], o_s.at[h], o_r.at[h], partner)

    def lse_copy(h):
        return remote(lse_send.at[h], lse_recv.at[h], l_s.at[h], l_r.at[h], partner)

    def vt_copy(h):
        return remote(vt.at[h], vtx.at[h], vt_s.at[h], vt_r.at[h], peer)

    kx_copy = remote(k_hbm, kx, kx_s, kx_r, peer)
    gives = place != 3
    takes = place != 2
    half_copy = remote(own_rows.at[1 - core], half_recv, st_s.at[0], st_r.at[0], peer)
    pair_copy = remote(half, pair_recv, st_s.at[1], st_r.at[1], partner)
    slot = table.at[core, :, pl.ds(pl.multiple_of((group * X + x) * SUMS, SUMS), SUMS), :]
    x_copies = [remote(slot, slot, x_s.at[n], x_r.at[n], to) for n, to in enumerate(along)]
    side = table.at[core, :, pl.ds(pl.multiple_of(group * X * SUMS, X * SUMS), X * SUMS), :]
    side_copy = remote(side, side, st_s.at[2], st_r.at[2], beside)
    table_copy = remote(table.at[core], table.at[core], st_s.at[3], st_r.at[3], peer)

    @pl.when(jnp.logical_not(first))
    def _():
        def send(h, _):
            q_copy(h).start()
            return 0

        lax.fori_loop(0, HEADS, send, 0)

    @pl.when(gives)
    def _():
        kx_copy.start()

    loads[0].wait()
    loads[1].wait()

    def turn(h, _):
        vt[h] = v[:, cols(h)].T

        @pl.when(gives)
        def _():
            vt_copy(h).start()

        return 0

    lax.fori_loop(0, HEADS, turn, 0)

    offset = lax.broadcasted_iota(jnp.int32, (SUMS, ROWS), 1) + place * ROWS
    row = lax.broadcasted_iota(jnp.int32, (SUMS, ROWS), 0)
    wanted = jnp.zeros((SUMS, ROWS), jnp.int32)
    for c in range(SUMS):
        wanted = jnp.where(row == c, pos_ref[stride, c], wanted)
    pick = jnp.where(offset == wanted, 1.0, 0.0).astype(jnp.bfloat16)

    def pick_rows(h, _):
        own_rows[0, h] = jnp.dot(pick, k[:, cols(h)], preferred_element_type=jnp.float32).astype(jnp.bfloat16)
        own_rows[1, h] = jnp.dot(pick, v[:, cols(h)], preferred_element_type=jnp.float32).astype(jnp.bfloat16)
        return 0

    lax.fori_loop(0, HEADS, pick_rows, 0)
    half_copy.start()
    loads[2].wait()

    key_id = lax.broadcasted_iota(jnp.int32, (ROWS, ROWS), 0)
    query_id = lax.broadcasted_iota(jnp.int32, (ROWS, ROWS), 1)

    def local(h):
        def keep(parts):
            total, top, weight = attend(parts, q[:, cols(h)])
            acc[h] = total
            acc_max[h] = top
            acc_sum[h] = weight

        @pl.when(core == 0)
        def _():
            keep([(k[:, cols(h)], vt[h], key_id <= query_id)])

        @pl.when(core == 1)
        def _():
            keep([(k[:, cols(h)], vt[h], key_id <= query_id), (kx[:, cols(h)], vtx[h], None)])

    def finish(h, remote_part):
        seen = lax.broadcasted_iota(jnp.int32, (STRIDES * SUMS, ROWS), 0) // SUMS
        seen = (seen % X) * 2 + seen // X < stride
        total, top, weight = attend([(table[0, h], table[1, h].T, seen)], q[:, cols(h)])
        high = jnp.maximum(top, acc_max[h])
        if remote_part:
            high = jnp.maximum(high, lse_recv[h])
        scale_sum = jnp.exp2(top - high)
        scale_own = jnp.exp2(acc_max[h] - high)
        top_part = total * scale_sum + acc[h] * scale_own
        low_part = weight * scale_sum + acc_sum[h] * scale_own
        if remote_part:
            scale_far = jnp.exp2(lse_recv[h] - high)
            top_part = top_part + o_recv[h].astype(jnp.float32) * scale_far
            low_part = low_part + scale_far
        staged[h] = (top_part / low_part).astype(jnp.bfloat16).T
        out_copy(h).start()

    def out_copy(h):
        return pltpu.make_async_copy(staged.at[h], out_hbm.at[:, cols(h)], out_sem.at[h])

    def stage_pair():
        half_copy.wait_recv()
        half[...] = own_rows[core] + half_recv[...]
        pair_copy.start()

    def stage_x():
        pair_copy.wait_recv()
        table[core, :, pl.ds(pl.multiple_of((group * X + x) * SUMS, SUMS), SUMS), :] = half[...] + pair_recv[...]
        for copy in x_copies:
            copy.start()

    def stage_side():
        for copy in x_copies:
            copy.wait_recv()
        side_copy.start()

    def stage_table():
        side_copy.wait_recv()
        table_copy.start()

    def step(h, _):
        @pl.when((h == 0) & takes)
        def _():
            kx_copy.wait_recv()

        @pl.when(takes)
        def _():
            vt_copy(h).wait_recv()

        local(h)
        pl.when(h == 0)(stage_pair)
        pl.when(h == 1)(stage_side)

        @pl.when(first)
        def _():
            q_copy(h).wait_recv()
            total, top, weight = attend(
                [(k[:, cols(h)], vt[h], None), (kx[:, cols(h)], vtx[h], None)], qr[h]
            )
            o_send[h] = (total / weight).astype(jnp.bfloat16)
            lse_send[h] = top + jnp.log2(weight)
            o_copy(h).start()
            lse_copy(h).start()

        pl.when(h == 0)(stage_x)
        pl.when(h == 1)(stage_table)

        @pl.when(h == 3)
        def _():
            table_copy.wait_recv()

        @pl.when(first & (h >= 4))
        def _():
            finish(2 * (h - 4), False)
            finish(2 * (h - 4) + 1, False)

        return 0

    lax.fori_loop(0, HEADS, step, 0)

    @pl.when(jnp.logical_not(first))
    def _():
        def merge(h, _):
            o_copy(h).wait_recv()
            lse_copy(h).wait_recv()
            finish(h, True)
            return 0

        lax.fori_loop(0, HEADS, merge, 0)

    def drain(h, _):
        out_copy(h).wait()

        @pl.when(gives)
        def _():
            vt_copy(h).wait_send()

        @pl.when(first)
        def _():
            o_copy(h).wait_send()
            lse_copy(h).wait_send()

        @pl.when(jnp.logical_not(first))
        def _():
            q_copy(h).wait_send()

        return 0

    lax.fori_loop(0, HEADS, drain, 0)

    @pl.when(gives)
    def _():
        kx_copy.wait_send()

    for copy in (half_copy, pair_copy, *x_copies, side_copy, table_copy):
        copy.wait_send()


def on_device(query_rows, key_rows, value_rows, summary_pos):
    bf16, f32 = jnp.bfloat16, jnp.float32
    dma = pltpu.SemaphoreType.DMA
    anywhere = pl.BlockSpec(memory_space=pl.ANY)
    per_head = dma((HEADS,))
    return pl.pallas_call(
        kernel,
        out_shape=jax.ShapeDtypeStruct(query_rows.shape, bf16),
        in_specs=[anywhere] * 3 + [pl.BlockSpec(memory_space=pltpu.SMEM)],
        out_specs=anywhere,
        scratch_shapes=[
            pltpu.VMEM((ROWS, HEADS * HD), bf16),
            pltpu.VMEM((ROWS, HEADS * HD), bf16),
            pltpu.VMEM((ROWS, HEADS * HD), bf16),
            pltpu.VMEM((ROWS, HEADS * HD), bf16),
            pltpu.VMEM((HEADS, HD, ROWS), bf16),
            pltpu.VMEM((HEADS, HD, ROWS), bf16),
            pltpu.VMEM((HEADS, ROWS, HD), bf16),
            pltpu.VMEM((HEADS, HD, ROWS), bf16),
            pltpu.VMEM((HEADS, HD, ROWS), bf16),
            pltpu.VMEM((HEADS, 1, ROWS), f32),
            pltpu.VMEM((HEADS, 1, ROWS), f32),
            pltpu.VMEM((HEADS, HD, ROWS), f32),
            pltpu.VMEM((HEADS, 1, ROWS), f32),
            pltpu.VMEM((HEADS, 1, ROWS), f32),
            pltpu.VMEM((HEADS, ROWS, HD), bf16),
            pltpu.VMEM((2, HEADS, SUMS, HD), bf16),
            pltpu.VMEM((HEADS, SUMS, HD), bf16),
            pltpu.VMEM((HEADS, SUMS, HD), bf16),
            pltpu.VMEM((HEADS, SUMS, HD), bf16),
            pltpu.VMEM((2, HEADS, STRIDES * SUMS, HD), bf16),
            dma((3,)),
            per_head, per_head,
            dma, dma,
            per_head, per_head,
            per_head, per_head,
            per_head, per_head,
            per_head,
            dma((4,)), dma((4,)),
            dma((X - 1,)), dma((X - 1,)),
        ],
        compiler_params=pltpu.CompilerParams(
            collective_id=0, has_side_effects=True, vmem_limit_bytes=56 * 2**20
        ),
    )(query_rows, key_rows, value_rows, summary_pos)


def solution(mesh):
    tokens = P(("dp", "ctx"), None)
    return jax.shard_map(
        on_device,
        mesh=mesh,
        in_specs=(tokens, tokens, tokens, P("dp", None)),
        out_specs=tokens,
        check_vma=False,
    )
```

```python
import functools

import jax
import jax.numpy as jnp
import numpy as np
from jax import lax
from jax.experimental import pallas as pl
from jax.experimental.pallas import tpu as pltpu
from jax.sharding import PartitionSpec as P

MESH = pl.DeviceIdType.MESH
HEADS = 8
HD = 128
ROWS = 512
SUMS = 16
STRIDES = 8
X = 4
RATE = float(HD**-0.5 * np.log2(np.e))
FLOOR = -1.0e30


def scores(keys, queries):
    return lax.dot_general(
        keys, queries, (((1,), (1,)), ((), ())), preferred_element_type=jnp.float32
    )


def attend(parts, queries):
    raw = []
    for keys, _, mask in parts:
        s = scores(keys, queries)
        raw.append(s if mask is None else jnp.where(mask, s, FLOOR))
    top = functools.reduce(jnp.maximum, [jnp.max(s, axis=0, keepdims=True) for s in raw]) * RATE
    total = None
    weight = None
    for s, (_, values, _) in zip(raw, parts):
        p = jnp.exp2(s * RATE - top)
        part_weight = jnp.sum(p, axis=0, keepdims=True)
        part = jnp.dot(values, p.astype(jnp.bfloat16), preferred_element_type=jnp.float32)
        total = part if total is None else total + part
        weight = part_weight if weight is None else weight + part_weight
    return total, top, weight


def kernel(
    q_hbm, k_hbm, v_hbm, pos_ref, out_hbm,
    q, k, v, kx, vt, vtx, qr, o_send, o_recv, lse_send, lse_recv,
    acc, acc_max, acc_sum, staged, own_rows, half_recv, half, pair_recv, table,
    load_sem, q_s, q_r, kx_s, kx_r, vt_s, vt_r, o_s, o_r, l_s, l_r, out_sem, st_s, st_r, x_s, x_r,
):
    me = lax.axis_index("ctx")
    core = me % 2
    y = (me // 2) % 4
    x = me // 8
    first = y % 2 == 0
    place = me % 4
    group = y // 2
    stride = x * 2 + group
    peer = me + 1 - 2 * core
    partner = jnp.where(first, me + 2, me - 2)
    beside = x * 8 + (jnp.where(first, y + 3, y + 1) % 4) * 2 + core
    along = [((x + d) % X) * 8 + y * 2 + core for d in range(1, X)]

    loads = [
        pltpu.make_async_copy(src, dst, load_sem.at[n])
        for n, (src, dst) in enumerate(((k_hbm, k), (v_hbm, v), (q_hbm, q)))
    ]
    for load in loads:
        load.start()

    barrier = pltpu.get_barrier_semaphore()
    for other in (peer, partner, beside, *along):
        pl.semaphore_signal(barrier, inc=1, device_id={"ctx": other}, device_id_type=MESH)
    pl.semaphore_wait(barrier, 6)

    def cols(h):
        return pl.ds(pl.multiple_of(h * HD, HD), HD)

    def remote(src, dst, s, r, to):
        return pltpu.make_async_remote_copy(
            src_ref=src, dst_ref=dst, send_sem=s, recv_sem=r, device_id={"ctx": to}, device_id_type=MESH
        )

    def q_copy(h):
        return remote(q_hbm.at[:, cols(h)], qr.at[h], q_s.at[h], q_r.at[h], partner)

    def o_copy(h):
        return remote(o_send.at[h], o_recv.at[h], o_s.at[h], o_r.at[h], partner)

    def lse_copy(h):
        return remote(lse_send.at[h], lse_recv.at[h], l_s.at[h], l_r.at[h], partner)

    def vt_copy(h):
        return remote(vt.at[h], vtx.at[h], vt_s.at[h], vt_r.at[h], peer)

    kx_copy = remote(k_hbm, kx, kx_s, kx_r, peer)
    gives = place != 3
    takes = place != 2
    half_copy = remote(own_rows.at[1 - core], half_recv, st_s.at[0], st_r.at[0], peer)
    pair_copy = remote(half, pair_recv, st_s.at[1], st_r.at[1], partner)
    slot = table.at[core, :, pl.ds(pl.multiple_of((group * X + x) * SUMS, SUMS), SUMS), :]
    x_copies = [remote(slot, slot, x_s.at[n], x_r.at[n], to) for n, to in enumerate(along)]
    side = table.at[core, :, pl.ds(pl.multiple_of(group * X * SUMS, X * SUMS), X * SUMS), :]
    side_copy = remote(side, side, st_s.at[2], st_r.at[2], beside)
    table_copy = remote(table.at[core], table.at[core], st_s.at[3], st_r.at[3], peer)

    @pl.when(jnp.logical_not(first))
    def _():
        q_copy(0).start()

    @pl.when(gives)
    def _():
        kx_copy.start()

    loads[0].wait()
    loads[1].wait()

    def stage_pair():
        half_copy.wait_recv()
        half[...] = own_rows[core] + half_recv[...]
        pair_copy.start()

    offset = lax.broadcasted_iota(jnp.int32, (SUMS, ROWS), 1) + place * ROWS
    row = lax.broadcasted_iota(jnp.int32, (SUMS, ROWS), 0)
    wanted = jnp.zeros((SUMS, ROWS), jnp.int32)
    for c in range(SUMS):
        wanted = jnp.where(row == c, pos_ref[stride, c], wanted)
    pick = jnp.where(offset == wanted, 1.0, 0.0).astype(jnp.bfloat16)

    for part, rows in enumerate((k, v)):
        picked = jnp.dot(pick, rows[...], preferred_element_type=jnp.float32).astype(jnp.bfloat16)
        for h in range(HEADS):
            own_rows[part, h] = picked[:, h * HD : (h + 1) * HD]
    half_copy.start()

    def turn(h, _):
        vt[h] = v[:, cols(h)].T

        @pl.when(gives)
        def _():
            vt_copy(h).start()

        return 0

    lax.fori_loop(0, HEADS, turn, 0)
    stage_pair()

    @pl.when(jnp.logical_not(first))
    def _():
        def send(h, _):
            q_copy(h).start()
            return 0

        lax.fori_loop(1, HEADS, send, 0)

    loads[2].wait()

    key_id = lax.broadcasted_iota(jnp.int32, (ROWS, ROWS), 0)
    query_id = lax.broadcasted_iota(jnp.int32, (ROWS, ROWS), 1)

    def local(h):
        def keep(parts):
            total, top, weight = attend(parts, q[:, cols(h)])
            acc[h] = total
            acc_max[h] = top
            acc_sum[h] = weight

        @pl.when(core == 0)
        def _():
            keep([(k[:, cols(h)], vt[h], key_id <= query_id)])

        @pl.when(core == 1)
        def _():
            keep([(k[:, cols(h)], vt[h], key_id <= query_id), (kx[:, cols(h)], vtx[h], None)])

    def finish(h, remote_part):
        seen = lax.broadcasted_iota(jnp.int32, (STRIDES * SUMS, ROWS), 0) // SUMS
        seen = (seen % X) * 2 + seen // X < stride
        total, top, weight = attend([(table[0, h], table[1, h].T, seen)], q[:, cols(h)])
        high = jnp.maximum(top, acc_max[h])
        if remote_part:
            high = jnp.maximum(high, lse_recv[h])
        scale_sum = jnp.exp2(top - high)
        scale_own = jnp.exp2(acc_max[h] - high)
        top_part = total * scale_sum + acc[h] * scale_own
        low_part = weight * scale_sum + acc_sum[h] * scale_own
        if remote_part:
            scale_far = jnp.exp2(lse_recv[h] - high)
            top_part = top_part + o_recv[h].astype(jnp.float32) * scale_far
            low_part = low_part + scale_far
        staged[h] = (top_part / low_part).astype(jnp.bfloat16).T
        out_copy(h).start()

    def out_copy(h):
        return pltpu.make_async_copy(staged.at[h], out_hbm.at[:, cols(h)], out_sem.at[h])

    def stage_x():
        pair_copy.wait_recv()
        table[core, :, pl.ds(pl.multiple_of((group * X + x) * SUMS, SUMS), SUMS), :] = half[...] + pair_recv[...]
        for copy in x_copies:
            copy.start()

    def stage_side():
        for copy in x_copies:
            copy.wait_recv()
        side_copy.start()

    def stage_table():
        side_copy.wait_recv()
        table_copy.start()

    def step(h, _):
        @pl.when((h == 0) & takes)
        def _():
            kx_copy.wait_recv()

        @pl.when(takes)
        def _():
            vt_copy(h).wait_recv()

        local(h)
        pl.when(h == 1)(stage_side)

        @pl.when(first)
        def _():
            q_copy(h).wait_recv()
            total, top, weight = attend(
                [(k[:, cols(h)], vt[h], None), (kx[:, cols(h)], vtx[h], None)], qr[h]
            )
            o_send[h] = (total / weight).astype(jnp.bfloat16)
            lse_send[h] = top + jnp.log2(weight)
            o_copy(h).start()
            lse_copy(h).start()

        pl.when(h == 0)(stage_x)
        pl.when(h == 1)(stage_table)

        @pl.when(h == 3)
        def _():
            table_copy.wait_recv()

        @pl.when(first & (h >= 4))
        def _():
            finish(2 * (h - 4), False)
            finish(2 * (h - 4) + 1, False)

        return 0

    lax.fori_loop(0, HEADS, step, 0)

    @pl.when(jnp.logical_not(first))
    def _():
        def merge(h, _):
            o_copy(h).wait_recv()
            lse_copy(h).wait_recv()
            finish(h, True)
            return 0

        lax.fori_loop(0, HEADS, merge, 0)

    def drain(h, _):
        out_copy(h).wait()

        @pl.when(gives)
        def _():
            vt_copy(h).wait_send()

        @pl.when(first)
        def _():
            o_copy(h).wait_send()
            lse_copy(h).wait_send()

        @pl.when(jnp.logical_not(first))
        def _():
            q_copy(h).wait_send()

        return 0

    lax.fori_loop(0, HEADS, drain, 0)

    @pl.when(gives)
    def _():
        kx_copy.wait_send()

    for copy in (half_copy, pair_copy, *x_copies, side_copy, table_copy):
        copy.wait_send()


def on_device(query_rows, key_rows, value_rows, summary_pos):
    bf16, f32 = jnp.bfloat16, jnp.float32
    dma = pltpu.SemaphoreType.DMA
    anywhere = pl.BlockSpec(memory_space=pl.ANY)
    per_head = dma((HEADS,))
    return pl.pallas_call(
        kernel,
        out_shape=jax.ShapeDtypeStruct(query_rows.shape, bf16),
        in_specs=[anywhere] * 3 + [pl.BlockSpec(memory_space=pltpu.SMEM)],
        out_specs=anywhere,
        scratch_shapes=[
            pltpu.VMEM((ROWS, HEADS * HD), bf16),
            pltpu.VMEM((ROWS, HEADS * HD), bf16),
            pltpu.VMEM((ROWS, HEADS * HD), bf16),
            pltpu.VMEM((ROWS, HEADS * HD), bf16),
            pltpu.VMEM((HEADS, HD, ROWS), bf16),
            pltpu.VMEM((HEADS, HD, ROWS), bf16),
            pltpu.VMEM((HEADS, ROWS, HD), bf16),
            pltpu.VMEM((HEADS, HD, ROWS), bf16),
            pltpu.VMEM((HEADS, HD, ROWS), bf16),
            pltpu.VMEM((HEADS, 1, ROWS), f32),
            pltpu.VMEM((HEADS, 1, ROWS), f32),
            pltpu.VMEM((HEADS, HD, ROWS), f32),
            pltpu.VMEM((HEADS, 1, ROWS), f32),
            pltpu.VMEM((HEADS, 1, ROWS), f32),
            pltpu.VMEM((HEADS, ROWS, HD), bf16),
            pltpu.VMEM((2, HEADS, SUMS, HD), bf16),
            pltpu.VMEM((HEADS, SUMS, HD), bf16),
            pltpu.VMEM((HEADS, SUMS, HD), bf16),
            pltpu.VMEM((HEADS, SUMS, HD), bf16),
            pltpu.VMEM((2, HEADS, STRIDES * SUMS, HD), bf16),
            dma((3,)),
            per_head, per_head,
            dma, dma,
            per_head, per_head,
            per_head, per_head,
            per_head, per_head,
            per_head,
            dma((4,)), dma((4,)),
            dma((X - 1,)), dma((X - 1,)),
        ],
        compiler_params=pltpu.CompilerParams(
            collective_id=0, has_side_effects=True, vmem_limit_bytes=52 * 2**20
        ),
    )(*(pltpu.with_memory_space_constraint(a, pltpu.HBM) for a in (query_rows, key_rows, value_rows, summary_pos)))


def solution(mesh):
    tokens = P(("dp", "ctx"), None)
    return jax.shard_map(
        on_device,
        mesh=mesh,
        in_specs=(tokens, tokens, tokens, P("dp", None)),
        out_specs=tokens,
        check_vma=False,
    )
```

```python
import functools

import jax
import jax.numpy as jnp
import numpy as np
from jax import lax
from jax.experimental import pallas as pl
from jax.experimental.pallas import tpu as pltpu
from jax.sharding import PartitionSpec as P

MESH = pl.DeviceIdType.MESH
HEADS = 8
HD = 128
ROWS = 512
SUMS = 16
STRIDES = 8
X = 4
RATE = float(HD**-0.5 * np.log2(np.e))
FLOOR = -1.0e30
KEPT = HEADS - 1


def scores(keys, queries):
    return lax.dot_general(
        keys, queries, (((1,), (1,)), ((), ())), preferred_element_type=jnp.float32
    )


def attend(parts, queries):
    raw = []
    for keys, _, mask in parts:
        s = scores(keys, queries)
        raw.append(s if mask is None else jnp.where(mask, s, FLOOR))
    top = functools.reduce(jnp.maximum, [jnp.max(s, axis=0, keepdims=True) for s in raw]) * RATE
    total = None
    weight = None
    for s, (_, values, _) in zip(raw, parts):
        p = jnp.exp2(s * RATE - top)
        part_weight = jnp.sum(p, axis=0, keepdims=True)
        part = jnp.dot(values, p.astype(jnp.bfloat16), preferred_element_type=jnp.float32)
        total = part if total is None else total + part
        weight = part_weight if weight is None else weight + part_weight
    return total, top, weight


def kernel(
    q_hbm, k_hbm, v_hbm, pos_ref, out_hbm,
    q, k, v, kx, vt, vtx, qr, o_send, o_recv, lse_send, lse_recv,
    acc, acc_max, acc_sum, staged, own_rows, rows_recv, chip_rows, pair_recv, table, kf, vf,
    load_sem, q_s, q_r, kx_s, kx_r, vt_s, vt_r, o_s, o_r, l_s, l_r, out_sem, st_s, st_r, x_s, x_r, f_s, f_r, ready,
):
    me = lax.axis_index("ctx")
    core = me % 2
    y = (me // 2) % 4
    x = me // 8
    first = y % 2 == 0
    second = y % 2 == 1
    hub = core == y % 2
    leaf = core != y % 2
    place = me % 4
    group = y // 2
    stride = x * 2 + group
    chip = me - core
    peer = chip + 1 - core
    partner = jnp.where(first, me + 2, me - 2)
    across = jnp.where(first, chip + 2, chip - 2) + 1 - core
    beside = x * 8 + (jnp.where(first, y + 3, y + 1) % 4) * 2 + 1 - core
    along = [((x + d) % X) * 8 + y * 2 + core for d in range(1, X)]

    loads = [
        pltpu.make_async_copy(src, dst, load_sem.at[n])
        for n, (src, dst) in enumerate(((k_hbm, k), (v_hbm, v), (q_hbm, q)))
    ]
    for load in loads:
        load.start()

    barrier = pltpu.get_barrier_semaphore()

    @pl.when(hub)
    def _():
        for other in (peer, partner, beside, *along):
            pl.semaphore_signal(barrier, inc=1, device_id={"ctx": other}, device_id_type=MESH)

    @pl.when(leaf)
    def _():
        pl.semaphore_wait(barrier, 2)
        pl.semaphore_signal(ready.at[0], inc=1, device_id={"ctx": peer}, device_id_type=MESH)
        pl.semaphore_signal(ready.at[1], inc=1, device_id={"ctx": partner}, device_id_type=MESH)

    @pl.when(hub)
    def _():
        pl.semaphore_wait(ready.at[0], 1)
        pl.semaphore_wait(ready.at[1], 1)

    def cols(h):
        return pl.ds(pl.multiple_of(h * HD, HD), HD)

    def remote(src, dst, s, r, to):
        return pltpu.make_async_remote_copy(
            src_ref=src, dst_ref=dst, send_sem=s, recv_sem=r, device_id={"ctx": to}, device_id_type=MESH
        )

    def q_copy(h):
        return remote(q_hbm.at[:, cols(h)], qr.at[h], q_s.at[h], q_r.at[h], partner)

    def o_copy(h):
        return remote(o_send.at[h], o_recv.at[h], o_s.at[h], o_r.at[h], partner)

    def lse_copy(h):
        return remote(lse_send.at[h], lse_recv.at[h], l_s.at[h], l_r.at[h], partner)

    def vt_copy(h):
        return remote(vt.at[h], vtx.at[h], vt_s.at[h], vt_r.at[h], peer)

    def out_copy(h):
        return pltpu.make_async_copy(staged.at[h], out_hbm.at[:, cols(h)], out_sem.at[h])

    kx_copy = remote(k_hbm, kx, kx_s, kx_r, peer)
    gives = place != 3
    takes = place != 2
    rows_copy = remote(own_rows, rows_recv, st_s.at[0], st_r.at[0], peer)
    pair_copy = remote(chip_rows, pair_recv, st_s.at[1], st_r.at[1], across)
    slot_rows = pl.ds(pl.multiple_of((group * X + x) * SUMS, SUMS), SUMS)
    slot = table.at[:, :, slot_rows, :]
    x_copies = [remote(slot, slot, x_s.at[n], x_r.at[n], to) for n, to in enumerate(along)]
    side = table.at[:, :, pl.ds(pl.multiple_of(group * X * SUMS, X * SUMS), X * SUMS), :]
    side_copy = remote(side, side, st_s.at[2], st_r.at[2], beside)
    table_copy = remote(table, table, st_s.at[3], st_r.at[3], peer)
    kf_copy = remote(k_hbm.at[:, KEPT * HD : HEADS * HD], kf.at[core], f_s.at[0], f_r.at[0], partner)
    vf_copy = remote(vt.at[KEPT], vf.at[core], f_s.at[1], f_r.at[1], partner)
    kf_pass = remote(kf.at[core], kf.at[core], f_s.at[2], f_r.at[2], peer)
    vf_pass = remote(vf.at[core], vf.at[core], f_s.at[3], f_r.at[3], peer)

    @pl.when(second)
    def _():
        q_copy(0).start()

    @pl.when(first)
    def _():
        kf_copy.start()

    @pl.when(gives)
    def _():
        kx_copy.start()

    def send_queries(h, _):
        q_copy(h).start()
        return 0

    @pl.when(second & leaf)
    def _():
        lax.fori_loop(1, KEPT, send_queries, 0)

    loads[0].wait()
    loads[1].wait()

    offset = lax.broadcasted_iota(jnp.int32, (SUMS, ROWS), 1) + place * ROWS
    row = lax.broadcasted_iota(jnp.int32, (SUMS, ROWS), 0)
    wanted = jnp.zeros((SUMS, ROWS), jnp.int32)
    for c in range(SUMS):
        wanted = jnp.where(row == c, pos_ref[stride, c], wanted)
    pick = jnp.where(offset == wanted, 1.0, 0.0).astype(jnp.bfloat16)

    for part, rows in enumerate((k, v)):
        picked = jnp.dot(pick, rows[...], preferred_element_type=jnp.float32).astype(jnp.bfloat16)
        for h in range(HEADS):
            own_rows[part, h] = picked[:, h * HD : (h + 1) * HD]

    @pl.when(leaf)
    def _():
        rows_copy.start()

    def turn(i, _):
        h = (i + KEPT) % HEADS
        vt[h] = v[:, cols(h)].T

        @pl.when(first & (i == 0))
        def _():
            vf_copy.start()

        @pl.when(gives)
        def _():
            vt_copy(h).start()

        return 0

    lax.fori_loop(0, HEADS, turn, 0)

    @pl.when(hub)
    def _():
        rows_copy.wait_recv()
        chip_rows[...] = own_rows[...] + rows_recv[...]
        pair_copy.start()

    @pl.when(second & hub)
    def _():
        lax.fori_loop(1, KEPT, send_queries, 0)

    loads[2].wait()

    key_id = lax.broadcasted_iota(jnp.int32, (ROWS, ROWS), 0)
    query_id = lax.broadcasted_iota(jnp.int32, (ROWS, ROWS), 1)

    def local(h):
        def keep(parts):
            total, top, weight = attend(parts, q[:, cols(h)])
            acc[h] = total
            acc_max[h] = top
            acc_sum[h] = weight

        @pl.when(core == 0)
        def _():
            keep([(k[:, cols(h)], vt[h], key_id <= query_id)])

        @pl.when(core == 1)
        def _():
            keep([(k[:, cols(h)], vt[h], key_id <= query_id), (kx[:, cols(h)], vtx[h], None)])

    def fold(h, total, top, weight):
        high = jnp.maximum(acc_max[h], top)
        scale_old = jnp.exp2(acc_max[h] - high)
        scale_new = jnp.exp2(top - high)
        return acc[h] * scale_old + total * scale_new, high, acc_sum[h] * scale_old + weight * scale_new

    def fold_summary(h):
        seen = lax.broadcasted_iota(jnp.int32, (STRIDES * SUMS, ROWS), 0) // SUMS
        seen = (seen % X) * 2 + seen // X < stride
        return fold(h, *attend([(table[0, h], table[1, h].T, seen)], q[:, cols(h)]))

    def put_out(h, total, weight):
        staged[h] = (total / weight).astype(jnp.bfloat16).T
        out_copy(h).start()

    def to_x():
        pair_copy.wait_recv()
        table[:, :, slot_rows, :] = chip_rows[...] + pair_recv[...]
        pl.semaphore_wait(barrier, 4)
        for copy in x_copies:
            copy.start()

    def to_side():
        for copy in x_copies:
            copy.wait_recv()
        side_copy.start()

    def to_peer():
        side_copy.wait_recv()
        table_copy.start()

    def step(h, _):
        @pl.when((h == 0) & takes)
        def _():
            kx_copy.wait_recv()

        @pl.when(takes)
        def _():
            vt_copy(h).wait_recv()

        @pl.when(first & (h < KEPT))
        def _():
            q_copy(h).wait_recv()
            total, top, weight = attend(
                [(k[:, cols(h)], vt[h], None), (kx[:, cols(h)], vtx[h], None)], qr[h]
            )
            o_send[h] = (total / weight).astype(jnp.bfloat16)
            lse_send[h] = top + jnp.log2(weight)
            lse_copy(h).start()
            o_copy(h).start()

        local(h)
        pl.when(hub & (h == jnp.where(first, 0, 2)))(to_x)
        pl.when(hub & (h == jnp.where(first, 2, 6)))(to_side)
        pl.when(hub & first & (h == 4))(to_peer)

        @pl.when(second & (h == 3))
        def _():
            kf_copy.wait_recv()
            vf_copy.wait_recv()
            kf_pass.start()
            vf_pass.start()

        return 0

    lax.fori_loop(0, HEADS, step, 0)
    pl.when(hub & second)(to_peer)

    @pl.when(second)
    def _():
        kf_pass.wait_recv()
        vf_pass.wait_recv()
        total, top, weight = fold(
            KEPT, *attend([(kf[0], vf[0], None), (kf[1], vf[1], None)], q[:, KEPT * HD : HEADS * HD])
        )
        acc[KEPT] = total
        acc_max[KEPT] = top
        acc_sum[KEPT] = weight

    @pl.when(leaf)
    def _():
        table_copy.wait_recv()

    @pl.when(first)
    def _():
        def close(h, _):
            total, _, weight = fold_summary(h)
            put_out(h, total, weight)
            return 0

        lax.fori_loop(0, HEADS, close, 0)

    @pl.when(second)
    def _():
        total, _, weight = fold_summary(KEPT)
        put_out(KEPT, total, weight)

        def close(h, _):
            total, top, weight = fold_summary(h)
            acc[h] = total
            lse_copy(h).wait_recv()
            o_copy(h).wait_recv()
            high = jnp.maximum(top, lse_recv[h])
            near = jnp.exp2(top - high)
            far = jnp.exp2(lse_recv[h] - high)
            put_out(h, acc[h] * near + o_recv[h].astype(jnp.float32) * far, weight * near + far)
            return 0

        lax.fori_loop(0, KEPT, close, 0)

    def drain(h, _):
        out_copy(h).wait()

        @pl.when(gives)
        def _():
            vt_copy(h).wait_send()

        @pl.when(first & (h < KEPT))
        def _():
            o_copy(h).wait_send()
            lse_copy(h).wait_send()

        @pl.when(second & (h < KEPT))
        def _():
            q_copy(h).wait_send()

        return 0

    lax.fori_loop(0, HEADS, drain, 0)

    @pl.when(gives)
    def _():
        kx_copy.wait_send()

    @pl.when(first)
    def _():
        kf_copy.wait_send()
        vf_copy.wait_send()

    @pl.when(second)
    def _():
        kf_pass.wait_send()
        vf_pass.wait_send()

    @pl.when(leaf)
    def _():
        rows_copy.wait_send()

    @pl.when(hub)
    def _():
        for copy in (pair_copy, *x_copies, side_copy, table_copy):
            copy.wait_send()


def on_device(query_rows, key_rows, value_rows, summary_pos):
    bf16, f32 = jnp.bfloat16, jnp.float32
    dma = pltpu.SemaphoreType.DMA
    anywhere = pl.BlockSpec(memory_space=pl.ANY)
    per_head = dma((HEADS,))
    return pl.pallas_call(
        kernel,
        out_shape=jax.ShapeDtypeStruct(query_rows.shape, bf16),
        in_specs=[anywhere] * 3 + [pl.BlockSpec(memory_space=pltpu.SMEM)],
        out_specs=anywhere,
        scratch_shapes=[
            pltpu.VMEM((ROWS, HEADS * HD), bf16),
            pltpu.VMEM((ROWS, HEADS * HD), bf16),
            pltpu.VMEM((ROWS, HEADS * HD), bf16),
            pltpu.VMEM((ROWS, HEADS * HD), bf16),
            pltpu.VMEM((HEADS, HD, ROWS), bf16),
            pltpu.VMEM((HEADS, HD, ROWS), bf16),
            pltpu.VMEM((HEADS, ROWS, HD), bf16),
            pltpu.VMEM((HEADS, HD, ROWS), bf16),
            pltpu.VMEM((HEADS, HD, ROWS), bf16),
            pltpu.VMEM((HEADS, 1, ROWS), f32),
            pltpu.VMEM((HEADS, 1, ROWS), f32),
            pltpu.VMEM((HEADS, HD, ROWS), f32),
            pltpu.VMEM((HEADS, 1, ROWS), f32),
            pltpu.VMEM((HEADS, 1, ROWS), f32),
            pltpu.VMEM((HEADS, ROWS, HD), bf16),
            pltpu.VMEM((2, HEADS, SUMS, HD), bf16),
            pltpu.VMEM((2, HEADS, SUMS, HD), bf16),
            pltpu.VMEM((2, HEADS, SUMS, HD), bf16),
            pltpu.VMEM((2, HEADS, SUMS, HD), bf16),
            pltpu.VMEM((2, HEADS, STRIDES * SUMS, HD), bf16),
            pltpu.VMEM((2, ROWS, HD), bf16),
            pltpu.VMEM((2, HD, ROWS), bf16),
            dma((3,)),
            per_head, per_head,
            dma, dma,
            per_head, per_head,
            per_head, per_head,
            per_head, per_head,
            per_head,
            dma((4,)), dma((4,)),
            dma((X - 1,)), dma((X - 1,)),
            dma((4,)), dma((4,)),
            pltpu.SemaphoreType.REGULAR((2,)),
        ],
        compiler_params=pltpu.CompilerParams(
            collective_id=0, has_side_effects=True, vmem_limit_bytes=52 * 2**20
        ),
    )(*(pltpu.with_memory_space_constraint(a, pltpu.HBM) for a in (query_rows, key_rows, value_rows, summary_pos)))


def solution(mesh):
    tokens = P(("dp", "ctx"), None)
    return jax.shard_map(
        on_device,
        mesh=mesh,
        in_specs=(tokens, tokens, tokens, P("dp", None)),
        out_specs=tokens,
        check_vma=False,
    )
```

```python
import jax
import jax.numpy as jnp
import numpy as np
from jax import lax
from jax.experimental import pallas as pl
from jax.experimental.pallas import tpu as pltpu
from jax.sharding import PartitionSpec as P

MESH = pl.DeviceIdType.MESH
HEADS = 8
HD = 128
ROWS = 512
SUMS = 16
STRIDES = 8
X = 4
RATE = float(HD**-0.5 * np.log2(np.e))
FLOOR = -1.0e30
KEPT = HEADS - 1


def scores(keys, queries):
    return lax.dot_general(
        keys, queries, (((1,), (1,)), ((), ())), preferred_element_type=jnp.float32
    )


def weigh(s):
    top = jnp.max(s, axis=0, keepdims=True) * RATE
    p = jnp.exp2(s * RATE - top)
    return p.astype(jnp.bfloat16), top, jnp.sum(p, axis=0, keepdims=True)


def mix(values, p):
    return jnp.dot(values, p, preferred_element_type=jnp.float32)


def attend(keys, values, queries, mask=None):
    s = scores(keys, queries)
    p, top, weight = weigh(s if mask is None else jnp.where(mask, s, FLOOR))
    return mix(values, p), top, weight


def attend_causal(keys, values, queries):
    half = ROWS // 2
    seen = lax.broadcasted_iota(jnp.int32, (half, half), 0) <= lax.broadcasted_iota(jnp.int32, (half, half), 1)
    early = scores(keys[:half], queries)
    late = jnp.where(seen, scores(keys[half:], queries[half:]), FLOOR)
    p, top, weight = weigh(jnp.where(seen, early[:, :half], FLOOR))
    low = mix(values[:, :half], p)
    p2, top2, weight2 = weigh(jnp.concatenate([early[:, half:], late], axis=0))
    high = mix(values, p2)
    return tuple(jnp.concatenate(pair, axis=1) for pair in ((low, high), (top, top2), (weight, weight2)))


def join(one, two):
    top = jnp.maximum(one[1], two[1])
    a, b = jnp.exp2(one[1] - top), jnp.exp2(two[1] - top)
    return one[0] * a + two[0] * b, top, one[2] * a + two[2] * b


def kernel(
    q_hbm, k_hbm, v_hbm, pos_ref, out_hbm,
    q, k, v, kx, vt, vtx, qr, o_send, o_recv, lse_send, lse_recv,
    acc, acc_max, acc_sum, staged, own_rows, rows_recv, chip_rows, pair_recv, table, kf, vf,
    load_sem, q_s, q_r, kx_s, kx_r, vt_s, vt_r, o_s, o_r, l_s, l_r, out_sem, st_s, st_r, x_s, x_r, f_s, f_r, ready,
):
    me = lax.axis_index("ctx")
    core = me % 2
    y = (me // 2) % 4
    x = me // 8
    first = y % 2 == 0
    second = y % 2 == 1
    hub = core == y % 2
    leaf = core != y % 2
    place = me % 4
    group = y // 2
    stride = x * 2 + group
    chip = me - core
    peer = chip + 1 - core
    partner = jnp.where(first, me + 2, me - 2)
    across = jnp.where(first, chip + 2, chip - 2) + 1 - core
    beside = x * 8 + (jnp.where(first, y + 3, y + 1) % 4) * 2 + 1 - core
    along = [((x + d) % X) * 8 + y * 2 + core for d in range(1, X)]

    loads = [
        pltpu.make_async_copy(src, dst, load_sem.at[n])
        for n, (src, dst) in enumerate(((k_hbm, k), (v_hbm, v), (q_hbm, q)))
    ]
    for load in loads:
        load.start()

    barrier = pltpu.get_barrier_semaphore()

    @pl.when(hub)
    def _():
        for other in (peer, partner, beside, *along):
            pl.semaphore_signal(barrier, inc=1, device_id={"ctx": other}, device_id_type=MESH)

    @pl.when(leaf)
    def _():
        pl.semaphore_signal(barrier, inc=1, device_id={"ctx": across}, device_id_type=MESH)
        pl.semaphore_wait(barrier, 3)
        pl.semaphore_signal(ready, inc=1, device_id={"ctx": peer}, device_id_type=MESH)

    @pl.when(hub)
    def _():
        pl.semaphore_wait(ready, 1)

    def cols(h):
        return pl.ds(pl.multiple_of(h * HD, HD), HD)

    def remote(src, dst, s, r, to):
        return pltpu.make_async_remote_copy(
            src_ref=src, dst_ref=dst, send_sem=s, recv_sem=r, device_id={"ctx": to}, device_id_type=MESH
        )

    def q_copy(h):
        return remote(q_hbm.at[:, cols(h)], qr.at[h], q_s.at[h], q_r.at[h], partner)

    def o_copy(h):
        return remote(o_send.at[h], o_recv.at[h], o_s.at[h], o_r.at[h], partner)

    def lse_copy(h):
        return remote(lse_send.at[h], lse_recv.at[h], l_s.at[h], l_r.at[h], partner)

    def vt_copy(h):
        return remote(vt.at[h], vtx.at[h], vt_s.at[h], vt_r.at[h], peer)

    def out_copy(h):
        return pltpu.make_async_copy(staged.at[h], out_hbm.at[:, cols(h)], out_sem.at[h])

    kx_copy = remote(k_hbm, kx, kx_s, kx_r, peer)
    gives = place != 3
    takes = place != 2
    rows_copy = remote(own_rows, rows_recv, st_s.at[0], st_r.at[0], peer)
    pair_copy = remote(chip_rows, pair_recv, st_s.at[1], st_r.at[1], across)
    slot_rows = pl.ds(pl.multiple_of((group * X + x) * SUMS, SUMS), SUMS)
    slot = table.at[:, :, slot_rows, :]
    x_copies = [remote(slot, slot, x_s.at[n], x_r.at[n], to) for n, to in enumerate(along)]
    side = table.at[:, :, pl.ds(pl.multiple_of(group * X * SUMS, X * SUMS), X * SUMS), :]
    side_copy = remote(side, side, st_s.at[2], st_r.at[2], beside)
    table_copy = remote(table, table, st_s.at[3], st_r.at[3], peer)
    kf_copy = remote(k_hbm.at[:, KEPT * HD : HEADS * HD], kf.at[core], f_s.at[0], f_r.at[0], partner)
    vf_copy = remote(vt.at[KEPT], vf.at[core], f_s.at[1], f_r.at[1], partner)
    kf_pass = remote(kf.at[core], kf.at[core], f_s.at[2], f_r.at[2], peer)
    vf_pass = remote(vf.at[core], vf.at[core], f_s.at[3], f_r.at[3], peer)

    @pl.when(second)
    def _():
        q_copy(0).start()

    @pl.when(first)
    def _():
        kf_copy.start()

    @pl.when(gives)
    def _():
        kx_copy.start()

    def send_queries(h, _):
        q_copy(h).start()
        return 0

    @pl.when(second & leaf)
    def _():
        lax.fori_loop(1, KEPT, send_queries, 0)

    loads[0].wait()
    loads[1].wait()

    offset = lax.broadcasted_iota(jnp.int32, (SUMS, ROWS), 1) + place * ROWS
    row = lax.broadcasted_iota(jnp.int32, (SUMS, ROWS), 0)
    wanted = jnp.zeros((SUMS, ROWS), jnp.int32)
    for c in range(SUMS):
        wanted = jnp.where(row == c, pos_ref[stride, c], wanted)
    pick = jnp.where(offset == wanted, 1.0, 0.0).astype(jnp.bfloat16)

    for part, rows in enumerate((k, v)):
        picked = jnp.dot(pick, rows[...], preferred_element_type=jnp.float32).astype(jnp.bfloat16)
        for h in range(HEADS):
            own_rows[part, h] = picked[:, h * HD : (h + 1) * HD]

    @pl.when(leaf)
    def _():
        rows_copy.start()

    def turn(i, _):
        h = (i + KEPT) % HEADS
        vt[h] = v[:, cols(h)].T

        @pl.when(first & (i == 0))
        def _():
            vf_copy.start()

        @pl.when(gives)
        def _():
            vt_copy(h).start()

        return 0

    lax.fori_loop(0, HEADS, turn, 0)

    @pl.when(hub)
    def _():
        rows_copy.wait_recv()
        chip_rows[...] = own_rows[...] + rows_recv[...]
        pair_copy.start()

    @pl.when(second & hub)
    def _():
        lax.fori_loop(1, KEPT, send_queries, 0)

    loads[2].wait()

    def local(h):
        return attend_causal(k[:, cols(h)], vt[h], q[:, cols(h)])

    def before(h):
        return attend(kx[:, cols(h)], vtx[h], q[:, cols(h)])

    def keep(h, part):
        acc[h], acc_max[h], acc_sum[h] = part

    def kept(h):
        return acc[h], acc_max[h], acc_sum[h]

    column = lax.broadcasted_iota(jnp.int32, (STRIDES * SUMS, 1), 0) // SUMS
    seen = (column % X) * 2 + column // X < stride

    def with_summary(h):
        return join(kept(h), attend(table[0, h], table[1, h].T, q[:, cols(h)], seen))

    def put_out(h, total, weight):
        staged[h] = (total * (1.0 / weight)).astype(jnp.bfloat16).T
        out_copy(h).start()

    def to_x():
        pair_copy.wait_recv()
        table[:, :, slot_rows, :] = chip_rows[...] + pair_recv[...]
        pl.semaphore_wait(barrier, 4)
        for copy in x_copies:
            copy.start()

    def to_side():
        for copy in x_copies:
            copy.wait_recv()
        side_copy.start()

    def to_peer():
        side_copy.wait_recv()
        table_copy.start()

    def wait_peer(h):
        @pl.when(h == 0)
        def _():
            kx_copy.wait_recv()

        vt_copy(h).wait_recv()

    def serve(h):
        queries = qr[h]
        total, top, weight = join(
            attend(k[:, cols(h)], vt[h], queries), attend(kx[:, cols(h)], vtx[h], queries)
        )
        o_send[h] = (total * (1.0 / weight)).astype(jnp.bfloat16)
        lse_send[h] = top + jnp.log2(weight)

    def reply(h):
        lse_copy(h).start()
        o_copy(h).start()

    def close(h):
        total, _, weight = with_summary(h)
        put_out(h, total, weight)

    @pl.when(first & hub)
    def _():
        def step(h, _):
            wait_peer(h)
            keep(h, local(h))

            @pl.when(h == 5)
            def _():
                to_peer()

            q_copy(h).wait_recv()
            serve(h)
            reply(h)
            pl.when(h == 1)(to_x)
            pl.when(h == 3)(to_side)
            return 0

        lax.fori_loop(0, KEPT, step, 0)
        wait_peer(KEPT)
        keep(KEPT, local(KEPT))

    @pl.when(first & leaf)
    def _():
        def step(h, _):
            wait_peer(h)
            keep(h, join(local(h), before(h)))

            q_copy(h).wait_recv()
            serve(h)
            reply(h)
            return 0

        lax.fori_loop(0, KEPT, step, 0)
        wait_peer(KEPT)
        keep(KEPT, join(local(KEPT), before(KEPT)))
        table_copy.wait_recv()

    def pass_on(i):
        @pl.when(i == 1)
        def _():
            kf_copy.wait_recv()
            vf_copy.wait_recv()
            kf_pass.start()
            vf_pass.start()

    @pl.when(second & leaf)
    def _():
        def step(i, _):
            h = 2 * i
            keep(h, local(h))
            keep(h + 1, local(h + 1))
            pass_on(i)
            return 0

        lax.fori_loop(0, HEADS // 2, step, 0)

    @pl.when(second & hub)
    def _():
        def step(i, _):
            h = 2 * i
            wait_peer(h)
            vt_copy(h + 1).wait_recv()
            keep(h, join(local(h), before(h)))
            keep(h + 1, join(local(h + 1), before(h + 1)))
            pl.when(i == 1)(to_x)
            pass_on(i)
            pl.when(i == 3)(to_side)
            return 0

        lax.fori_loop(0, HEADS // 2, step, 0)

    @pl.when(first)
    def _():
        def closes(i, _):
            close(2 * i)
            close(2 * i + 1)
            return 0

        lax.fori_loop(0, HEADS // 2, closes, 0)

    @pl.when(second)
    def _():
        kf_pass.wait_recv()
        vf_pass.wait_recv()
        queries = q[:, KEPT * HD : HEADS * HD]
        far = join(attend(kf[0], vf[0], queries), attend(kf[1], vf[1], queries))
        keep(KEPT, join(kept(KEPT), far))
        pl.when(hub)(to_peer)

        @pl.when(leaf)
        def _():
            table_copy.wait_recv()

        close(KEPT)

        def finish(h, _):
            keep(h, with_summary(h))
            lse_copy(h).wait_recv()
            o_copy(h).wait_recv()
            total, _, weight = join(kept(h), (o_recv[h].astype(jnp.float32), lse_recv[h], 1.0))
            put_out(h, total, weight)
            return 0

        lax.fori_loop(0, KEPT, finish, 0)

    def drain(h, _):
        out_copy(h).wait()

        @pl.when(gives)
        def _():
            vt_copy(h).wait_send()

        @pl.when(first & (h < KEPT))
        def _():
            o_copy(h).wait_send()
            lse_copy(h).wait_send()

        @pl.when(second & (h < KEPT))
        def _():
            q_copy(h).wait_send()

        return 0

    lax.fori_loop(0, HEADS, drain, 0)

    @pl.when(gives)
    def _():
        kx_copy.wait_send()

    @pl.when(first)
    def _():
        kf_copy.wait_send()
        vf_copy.wait_send()

    @pl.when(second)
    def _():
        kf_pass.wait_send()
        vf_pass.wait_send()

    @pl.when(leaf)
    def _():
        rows_copy.wait_send()

    @pl.when(hub)
    def _():
        for copy in (pair_copy, *x_copies, side_copy, table_copy):
            copy.wait_send()


def on_device(query_rows, key_rows, value_rows, summary_pos):
    bf16, f32 = jnp.bfloat16, jnp.float32
    dma = pltpu.SemaphoreType.DMA
    anywhere = pl.BlockSpec(memory_space=pl.ANY)
    per_head = dma((HEADS,))
    return pl.pallas_call(
        kernel,
        out_shape=jax.ShapeDtypeStruct(query_rows.shape, bf16),
        in_specs=[anywhere] * 3 + [pl.BlockSpec(memory_space=pltpu.SMEM)],
        out_specs=anywhere,
        scratch_shapes=[
            pltpu.VMEM((ROWS, HEADS * HD), bf16),
            pltpu.VMEM((ROWS, HEADS * HD), bf16),
            pltpu.VMEM((ROWS, HEADS * HD), bf16),
            pltpu.VMEM((ROWS, HEADS * HD), bf16),
            pltpu.VMEM((HEADS, HD, ROWS), bf16),
            pltpu.VMEM((HEADS, HD, ROWS), bf16),
            pltpu.VMEM((HEADS, ROWS, HD), bf16),
            pltpu.VMEM((HEADS, HD, ROWS), bf16),
            pltpu.VMEM((HEADS, HD, ROWS), bf16),
            pltpu.VMEM((HEADS, 1, ROWS), f32),
            pltpu.VMEM((HEADS, 1, ROWS), f32),
            pltpu.VMEM((HEADS, HD, ROWS), f32),
            pltpu.VMEM((HEADS, 1, ROWS), f32),
            pltpu.VMEM((HEADS, 1, ROWS), f32),
            pltpu.VMEM((HEADS, ROWS, HD), bf16),
            pltpu.VMEM((2, HEADS, SUMS, HD), bf16),
            pltpu.VMEM((2, HEADS, SUMS, HD), bf16),
            pltpu.VMEM((2, HEADS, SUMS, HD), bf16),
            pltpu.VMEM((2, HEADS, SUMS, HD), bf16),
            pltpu.VMEM((2, HEADS, STRIDES * SUMS, HD), bf16),
            pltpu.VMEM((2, ROWS, HD), bf16),
            pltpu.VMEM((2, HD, ROWS), bf16),
            dma((3,)),
            per_head, per_head,
            dma, dma,
            per_head, per_head,
            per_head, per_head,
            per_head, per_head,
            per_head,
            dma((4,)), dma((4,)),
            dma((X - 1,)), dma((X - 1,)),
            dma((4,)), dma((4,)),
            pltpu.SemaphoreType.REGULAR,
        ],
        compiler_params=pltpu.CompilerParams(
            collective_id=0, has_side_effects=True, vmem_limit_bytes=52 * 2**20
        ),
    )(*(pltpu.with_memory_space_constraint(a, pltpu.HBM) for a in (query_rows, key_rows, value_rows, summary_pos)))


def solution(mesh):
    tokens = P(("dp", "ctx"), None)
    return jax.shard_map(
        on_device,
        mesh=mesh,
        in_specs=(tokens, tokens, tokens, P("dp", None)),
        out_specs=tokens,
        check_vma=False,
    )
```

```python
import jax
import jax.numpy as jnp
import numpy as np
from jax import lax
from jax.experimental import pallas as pl
from jax.experimental.pallas import tpu as pltpu
from jax.sharding import PartitionSpec as P

MESH = pl.DeviceIdType.MESH
HEADS = 8
HD = 128
ROWS = 512
SUMS = 16
STRIDES = 8
X = 4
RATE = float(HD**-0.5 * np.log2(np.e))
FLOOR = -1.0e30
KEPT = HEADS - 1


def scores(keys, queries):
    return lax.dot_general(
        keys, queries, (((1,), (1,)), ((), ())), preferred_element_type=jnp.float32
    )


def weigh(s):
    top = jnp.max(s, axis=0, keepdims=True) * RATE
    p = jnp.exp2(s * RATE - top)
    return p.astype(jnp.bfloat16), top, jnp.sum(p, axis=0, keepdims=True)


def mix(values, p):
    return jnp.dot(values, p, preferred_element_type=jnp.float32)


def attend(keys, values, queries, mask=None):
    s = scores(keys, queries)
    p, top, weight = weigh(s if mask is None else jnp.where(mask, s, FLOOR))
    return mix(values, p), top, weight


def attend_causal(keys, values, queries):
    half = ROWS // 2
    seen = lax.broadcasted_iota(jnp.int32, (half, half), 0) <= lax.broadcasted_iota(jnp.int32, (half, half), 1)
    early = scores(keys[:half], queries)
    late = jnp.where(seen, scores(keys[half:], queries[half:]), FLOOR)
    p, top, weight = weigh(jnp.where(seen, early[:, :half], FLOOR))
    low = mix(values[:, :half], p)
    p2, top2, weight2 = weigh(jnp.concatenate([early[:, half:], late], axis=0))
    high = mix(values, p2)
    return tuple(jnp.concatenate(pair, axis=1) for pair in ((low, high), (top, top2), (weight, weight2)))


def join(one, two):
    top = jnp.maximum(one[1], two[1])
    a, b = jnp.exp2(one[1] - top), jnp.exp2(two[1] - top)
    return one[0] * a + two[0] * b, top, one[2] * a + two[2] * b


def kernel(
    q_hbm, k_hbm, v_hbm, pos_ref, out_hbm,
    q, k, v, kx, vt, vtx, qr, o_send, o_recv, lse_send, lse_recv,
    acc, acc_max, acc_sum, staged, own_rows, rows_recv, chip_rows, pair_recv, table, kf, vf,
    load_sem, q_s, q_r, kx_s, kx_r, vt_s, vt_r, o_s, o_r, l_s, l_r, out_sem, st_s, st_r, x_s, x_r, f_s, f_r, ready,
):
    me = lax.axis_index("ctx")
    core = me % 2
    y = (me // 2) % 4
    x = me // 8
    first = y % 2 == 0
    second = y % 2 == 1
    hub = core == y % 2
    leaf = core != y % 2
    place = me % 4
    group = y // 2
    stride = x * 2 + group
    chip = me - core
    peer = chip + 1 - core
    partner = jnp.where(first, me + 2, me - 2)
    across = jnp.where(first, chip + 2, chip - 2) + 1 - core
    beside = x * 8 + (jnp.where(first, y + 3, y + 1) % 4) * 2 + 1 - core
    along = [((x + d) % X) * 8 + y * 2 + core for d in range(1, X)]

    barrier = pltpu.get_barrier_semaphore()

    @pl.when(hub)
    def _():
        for other in (peer, partner, beside, *along):
            pl.semaphore_signal(barrier, inc=1, device_id={"ctx": other}, device_id_type=MESH)

    loads = [
        pltpu.make_async_copy(src, dst, load_sem.at[n])
        for n, (src, dst) in enumerate(((k_hbm, k), (v_hbm, v), (q_hbm, q)))
    ]
    for load in loads:
        load.start()

    @pl.when(leaf)
    def _():
        pl.semaphore_signal(barrier, inc=1, device_id={"ctx": across}, device_id_type=MESH)
        pl.semaphore_wait(barrier, 3)
        pl.semaphore_signal(ready, inc=1, device_id={"ctx": peer}, device_id_type=MESH)

    @pl.when(hub)
    def _():
        pl.semaphore_wait(ready, 1)

    def cols(h):
        return pl.ds(pl.multiple_of(h * HD, HD), HD)

    def remote(src, dst, s, r, to):
        return pltpu.make_async_remote_copy(
            src_ref=src, dst_ref=dst, send_sem=s, recv_sem=r, device_id={"ctx": to}, device_id_type=MESH
        )

    def q_copy(h):
        return remote(q_hbm.at[:, cols(h)], qr.at[h], q_s.at[h], q_r.at[h], partner)

    def o_copy(h):
        return remote(o_send.at[h], o_recv.at[h], o_s.at[h], o_r.at[h], partner)

    def lse_copy(h):
        return remote(lse_send.at[h], lse_recv.at[h], l_s.at[h], l_r.at[h], partner)

    def vt_copy(h):
        return remote(vt.at[h], vtx.at[h], vt_s.at[h], vt_r.at[h], peer)

    def out_copy(h):
        return pltpu.make_async_copy(staged.at[h], out_hbm.at[:, cols(h)], out_sem.at[h])

    kx_copy = remote(k_hbm, kx, kx_s, kx_r, peer)
    gives = place != 3
    takes = place != 2
    rows_copy = remote(own_rows, rows_recv, st_s.at[0], st_r.at[0], peer)
    pair_copy = remote(chip_rows, pair_recv, st_s.at[1], st_r.at[1], across)
    slot_rows = pl.ds(pl.multiple_of((group * X + x) * SUMS, SUMS), SUMS)
    slot = table.at[:, :, slot_rows, :]
    x_copies = [remote(slot, slot, x_s.at[n], x_r.at[n], to) for n, to in enumerate(along)]
    side = table.at[:, :, pl.ds(pl.multiple_of(group * X * SUMS, X * SUMS), X * SUMS), :]
    side_copy = remote(side, side, st_s.at[2], st_r.at[2], beside)
    table_copy = remote(table, table, st_s.at[3], st_r.at[3], peer)
    kf_copy = remote(k_hbm.at[:, KEPT * HD : HEADS * HD], kf.at[core], f_s.at[0], f_r.at[0], partner)
    vf_copy = remote(vt.at[KEPT], vf.at[core], f_s.at[1], f_r.at[1], partner)
    kf_pass = remote(kf.at[core], kf.at[core], f_s.at[2], f_r.at[2], peer)
    vf_pass = remote(vf.at[core], vf.at[core], f_s.at[3], f_r.at[3], peer)

    @pl.when(second)
    def _():
        q_copy(0).start()

    @pl.when(first)
    def _():
        kf_copy.start()

    @pl.when(gives)
    def _():
        kx_copy.start()

    def send_queries(h, _):
        q_copy(h).start()
        return 0

    @pl.when(second & leaf)
    def _():
        lax.fori_loop(1, KEPT, send_queries, 0)

    loads[0].wait()
    loads[1].wait()

    offset = lax.broadcasted_iota(jnp.int32, (SUMS, ROWS), 1) + place * ROWS
    row = lax.broadcasted_iota(jnp.int32, (SUMS, ROWS), 0)
    wanted = jnp.zeros((SUMS, ROWS), jnp.int32)
    for c in range(SUMS):
        wanted = jnp.where(row == c, pos_ref[stride, c], wanted)
    pick = jnp.where(offset == wanted, 1.0, 0.0).astype(jnp.bfloat16)

    for part, rows in enumerate((k, v)):
        picked = jnp.dot(pick, rows[...], preferred_element_type=jnp.float32).astype(jnp.bfloat16)
        for h in range(HEADS):
            own_rows[part, h] = picked[:, h * HD : (h + 1) * HD]

    @pl.when(leaf)
    def _():
        rows_copy.start()

    def turn(i, _):
        h = (i + KEPT) % HEADS
        vt[h] = v[:, cols(h)].T

        @pl.when(first & (i == 0))
        def _():
            vf_copy.start()

        @pl.when(gives)
        def _():
            vt_copy(h).start()

        return 0

    lax.fori_loop(0, HEADS, turn, 0)

    @pl.when(hub)
    def _():
        rows_copy.wait_recv()
        chip_rows[...] = own_rows[...] + rows_recv[...]
        pair_copy.start()

    @pl.when(second & hub)
    def _():
        lax.fori_loop(1, KEPT, send_queries, 0)

    loads[2].wait()

    def local(h):
        return attend_causal(k[:, cols(h)], vt[h], q[:, cols(h)])

    def before(h):
        return attend(kx[:, cols(h)], vtx[h], q[:, cols(h)])

    def keep(h, part):
        acc[h], acc_max[h], acc_sum[h] = part

    def kept(h):
        return acc[h], acc_max[h], acc_sum[h]

    column = lax.broadcasted_iota(jnp.int32, (STRIDES * SUMS, 1), 0) // SUMS
    seen = (column % X) * 2 + column // X < stride

    def with_summary(h):
        return join(kept(h), attend(table[0, h], table[1, h].T, q[:, cols(h)], seen))

    def put_out(h, total, weight):
        staged[h] = (total * (1.0 / weight)).astype(jnp.bfloat16).T
        out_copy(h).start()

    def to_x():
        pair_copy.wait_recv()
        table[:, :, slot_rows, :] = chip_rows[...] + pair_recv[...]
        pl.semaphore_wait(barrier, 4)
        for copy in x_copies:
            copy.start()

    def to_side():
        for copy in x_copies:
            copy.wait_recv()
        side_copy.start()

    def to_peer():
        side_copy.wait_recv()
        table_copy.start()

    def wait_peer(h):
        @pl.when(h == 0)
        def _():
            kx_copy.wait_recv()

        vt_copy(h).wait_recv()

    def serve(h):
        queries = qr[h]
        total, top, weight = join(
            attend(k[:, cols(h)], vt[h], queries), attend(kx[:, cols(h)], vtx[h], queries)
        )
        o_send[h] = (total * (1.0 / weight)).astype(jnp.bfloat16)
        lse_send[h] = top + jnp.log2(weight)

    def reply(h):
        lse_copy(h).start()
        o_copy(h).start()

    def close(h):
        total, _, weight = with_summary(h)
        put_out(h, total, weight)

    @pl.when(first & hub)
    def _():
        def step(h, _):
            wait_peer(h)
            keep(h, local(h))

            @pl.when(h == 3)
            def _():
                vt_copy(KEPT).wait_recv()
                keep(KEPT, local(KEPT))

            @pl.when(h == 5)
            def _():
                to_peer()

            q_copy(h).wait_recv()
            serve(h)
            reply(h)
            pl.when(h == 1)(to_x)
            pl.when(h == 3)(to_side)
            return 0

        lax.fori_loop(0, KEPT, step, 0)

    @pl.when(first & leaf)
    def _():
        def step(h, _):
            @pl.when(h == 4)
            def _():
                vt_copy(KEPT).wait_recv()
                keep(KEPT, join(local(KEPT), before(KEPT)))

            wait_peer(h)
            keep(h, join(local(h), before(h)))

            q_copy(h).wait_recv()
            serve(h)
            reply(h)
            return 0

        lax.fori_loop(0, KEPT, step, 0)
        table_copy.wait_recv()

    def pass_on(i):
        @pl.when(i == 1)
        def _():
            kf_copy.wait_recv()
            vf_copy.wait_recv()
            kf_pass.start()
            vf_pass.start()

    @pl.when(second & leaf)
    def _():
        def step(i, _):
            h = 2 * i
            keep(h, local(h))
            keep(h + 1, local(h + 1))
            pass_on(i)
            return 0

        lax.fori_loop(0, HEADS // 2, step, 0)

    @pl.when(second & hub)
    def _():
        def step(i, _):
            h = 2 * i
            wait_peer(h)
            vt_copy(h + 1).wait_recv()
            keep(h, join(local(h), before(h)))
            keep(h + 1, join(local(h + 1), before(h + 1)))
            pl.when(i == 1)(to_x)
            pass_on(i)
            pl.when(i == 3)(to_side)
            return 0

        lax.fori_loop(0, HEADS // 2, step, 0)

    @pl.when(first)
    def _():
        def closes(i, _):
            for n in range(4):
                close(4 * i + n)
            return 0

        lax.fori_loop(0, HEADS // 4, closes, 0)

    @pl.when(second)
    def _():
        kf_pass.wait_recv()
        vf_pass.wait_recv()
        queries = q[:, KEPT * HD : HEADS * HD]
        far = join(attend(kf[0], vf[0], queries), attend(kf[1], vf[1], queries))
        keep(KEPT, join(kept(KEPT), far))
        pl.when(hub)(to_peer)

        @pl.when(leaf)
        def _():
            table_copy.wait_recv()

        close(KEPT)

        def finish(h, _):
            keep(h, with_summary(h))
            lse_copy(h).wait_recv()
            o_copy(h).wait_recv()
            total, _, weight = join(kept(h), (o_recv[h].astype(jnp.float32), lse_recv[h], 1.0))
            put_out(h, total, weight)
            return 0

        lax.fori_loop(0, KEPT, finish, 0)

    def drain(h, _):
        out_copy(h).wait()

        @pl.when(gives)
        def _():
            vt_copy(h).wait_send()

        @pl.when(first & (h < KEPT))
        def _():
            o_copy(h).wait_send()
            lse_copy(h).wait_send()

        @pl.when(second & (h < KEPT))
        def _():
            q_copy(h).wait_send()

        return 0

    lax.fori_loop(0, HEADS, drain, 0)

    @pl.when(gives)
    def _():
        kx_copy.wait_send()

    @pl.when(first)
    def _():
        kf_copy.wait_send()
        vf_copy.wait_send()

    @pl.when(second)
    def _():
        kf_pass.wait_send()
        vf_pass.wait_send()

    @pl.when(leaf)
    def _():
        rows_copy.wait_send()

    @pl.when(hub)
    def _():
        for copy in (pair_copy, *x_copies, side_copy, table_copy):
            copy.wait_send()


def on_device(query_rows, key_rows, value_rows, summary_pos):
    bf16, f32 = jnp.bfloat16, jnp.float32
    dma = pltpu.SemaphoreType.DMA
    anywhere = pl.BlockSpec(memory_space=pl.ANY)
    per_head = dma((HEADS,))
    return pl.pallas_call(
        kernel,
        out_shape=jax.ShapeDtypeStruct(query_rows.shape, bf16),
        in_specs=[anywhere] * 3 + [pl.BlockSpec(memory_space=pltpu.SMEM)],
        out_specs=anywhere,
        scratch_shapes=[
            pltpu.VMEM((ROWS, HEADS * HD), bf16),
            pltpu.VMEM((ROWS, HEADS * HD), bf16),
            pltpu.VMEM((ROWS, HEADS * HD), bf16),
            pltpu.VMEM((ROWS, HEADS * HD), bf16),
            pltpu.VMEM((HEADS, HD, ROWS), bf16),
            pltpu.VMEM((HEADS, HD, ROWS), bf16),
            pltpu.VMEM((HEADS, ROWS, HD), bf16),
            pltpu.VMEM((HEADS, HD, ROWS), bf16),
            pltpu.VMEM((HEADS, HD, ROWS), bf16),
            pltpu.VMEM((HEADS, 1, ROWS), f32),
            pltpu.VMEM((HEADS, 1, ROWS), f32),
            pltpu.VMEM((HEADS, HD, ROWS), f32),
            pltpu.VMEM((HEADS, 1, ROWS), f32),
            pltpu.VMEM((HEADS, 1, ROWS), f32),
            pltpu.VMEM((HEADS, ROWS, HD), bf16),
            pltpu.VMEM((2, HEADS, SUMS, HD), bf16),
            pltpu.VMEM((2, HEADS, SUMS, HD), bf16),
            pltpu.VMEM((2, HEADS, SUMS, HD), bf16),
            pltpu.VMEM((2, HEADS, SUMS, HD), bf16),
            pltpu.VMEM((2, HEADS, STRIDES * SUMS, HD), bf16),
            pltpu.VMEM((2, ROWS, HD), bf16),
            pltpu.VMEM((2, HD, ROWS), bf16),
            dma((3,)),
            per_head, per_head,
            dma, dma,
            per_head, per_head,
            per_head, per_head,
            per_head, per_head,
            per_head,
            dma((4,)), dma((4,)),
            dma((X - 1,)), dma((X - 1,)),
            dma((4,)), dma((4,)),
            pltpu.SemaphoreType.REGULAR,
        ],
        compiler_params=pltpu.CompilerParams(
            collective_id=0, has_side_effects=True, vmem_limit_bytes=52 * 2**20
        ),
    )(*(pltpu.with_memory_space_constraint(a, pltpu.HBM) for a in (query_rows, key_rows, value_rows, summary_pos)))


def solution(mesh):
    tokens = P(("dp", "ctx"), None)
    return jax.shard_map(
        on_device,
        mesh=mesh,
        in_specs=(tokens, tokens, tokens, P("dp", None)),
        out_specs=tokens,
        check_vma=False,
    )
```

```python
import jax
import jax.numpy as jnp
import numpy as np
from jax import lax
from jax.experimental import pallas as pl
from jax.experimental.pallas import tpu as pltpu
from jax.sharding import PartitionSpec as P

MESH = pl.DeviceIdType.MESH
HEADS = 8
HD = 128
ROWS = 512
SUMS = 16
STRIDES = 8
X = 4
RATE = float(HD**-0.5 * np.log2(np.e))
FLOOR = -1.0e30
KEPT = HEADS - 1


def scores(keys, queries):
    return lax.dot_general(
        keys, queries, (((1,), (1,)), ((), ())), preferred_element_type=jnp.float32
    )


def weigh(s):
    top = jnp.max(s, axis=0, keepdims=True) * RATE
    p = jnp.exp2(s * RATE - top)
    return p.astype(jnp.bfloat16), top, jnp.sum(p, axis=0, keepdims=True)


def mix(values, p):
    return jnp.dot(values, p, preferred_element_type=jnp.float32)


def attend(keys, values, queries, mask=None):
    s = scores(keys, queries)
    p, top, weight = weigh(s if mask is None else jnp.where(mask, s, FLOOR))
    return mix(values, p), top, weight


def attend_causal(keys, values, queries):
    half = ROWS // 2
    seen = lax.broadcasted_iota(jnp.int32, (half, half), 0) <= lax.broadcasted_iota(jnp.int32, (half, half), 1)
    early = scores(keys[:half], queries)
    late = jnp.where(seen, scores(keys[half:], queries[half:]), FLOOR)
    p, top, weight = weigh(jnp.where(seen, early[:, :half], FLOOR))
    low = mix(values[:, :half], p)
    p2, top2, weight2 = weigh(jnp.concatenate([early[:, half:], late], axis=0))
    high = mix(values, p2)
    return tuple(jnp.concatenate(pair, axis=1) for pair in ((low, high), (top, top2), (weight, weight2)))


def join(one, two):
    top = jnp.maximum(one[1], two[1])
    a, b = jnp.exp2(one[1] - top), jnp.exp2(two[1] - top)
    return one[0] * a + two[0] * b, top, one[2] * a + two[2] * b


def kernel(
    q_hbm, k_hbm, v_hbm, pos_ref, out_hbm,
    q, k, v, kx, vt, vtx, qr, o_send, o_recv, lse_send, lse_recv,
    acc, acc_max, acc_sum, staged, own_rows, rows_recv, chip_rows, pair_recv, table, kf, vf,
    load_sem, q_s, q_r, kx_s, kx_r, vt_s, vt_r, o_s, o_r, l_s, l_r, out_sem, st_s, st_r, x_s, x_r, f_s, f_r, ready,
):
    me = lax.axis_index("ctx")
    core = me % 2
    y = (me // 2) % 4
    x = me // 8
    first = y % 2 == 0
    second = y % 2 == 1
    hub = core == y % 2
    leaf = core != y % 2
    place = me % 4
    group = y // 2
    stride = x * 2 + group
    chip = me - core
    peer = chip + 1 - core
    partner = jnp.where(first, me + 2, me - 2)
    across = jnp.where(first, chip + 2, chip - 2) + 1 - core
    beside = x * 8 + (jnp.where(first, y + 3, y + 1) % 4) * 2 + 1 - core
    along = [((x + d) % X) * 8 + y * 2 + core for d in range(1, X)]

    barrier = pltpu.get_barrier_semaphore()

    @pl.when(hub)
    def _():
        for other in (peer, partner, beside, *along):
            pl.semaphore_signal(barrier, inc=1, device_id={"ctx": other}, device_id_type=MESH)

    loads = [
        pltpu.make_async_copy(src, dst, load_sem.at[n])
        for n, (src, dst) in enumerate(((k_hbm, k), (v_hbm, v), (q_hbm, q)))
    ]
    for load in loads:
        load.start()

    @pl.when(leaf)
    def _():
        pl.semaphore_signal(barrier, inc=1, device_id={"ctx": across}, device_id_type=MESH)
        pl.semaphore_wait(barrier, 3)
        pl.semaphore_signal(ready, inc=1, device_id={"ctx": peer}, device_id_type=MESH)

    @pl.when(hub)
    def _():
        pl.semaphore_wait(ready, 1)

    def cols(h):
        return pl.ds(pl.multiple_of(h * HD, HD), HD)

    def remote(src, dst, s, r, to):
        return pltpu.make_async_remote_copy(
            src_ref=src, dst_ref=dst, send_sem=s, recv_sem=r, device_id={"ctx": to}, device_id_type=MESH
        )

    def q_copy(h):
        return remote(q_hbm.at[:, cols(h)], qr.at[h], q_s.at[h], q_r.at[h], partner)

    def o_copy(h):
        return remote(o_send.at[h], o_recv.at[h], o_s.at[h], o_r.at[h], partner)

    def lse_copy(h):
        return remote(lse_send.at[h], lse_recv.at[h], l_s.at[h], l_r.at[h], partner)

    def vt_copy(h):
        return remote(vt.at[h], vtx.at[h], vt_s.at[h], vt_r.at[h], peer)

    def out_copy(h):
        return pltpu.make_async_copy(staged.at[h], out_hbm.at[:, cols(h)], out_sem.at[h])

    kx_copy = remote(k_hbm, kx, kx_s, kx_r, peer)
    gives = place != 3
    takes = place != 2
    rows_copy = remote(own_rows, rows_recv, st_s.at[0], st_r.at[0], peer)
    pair_copy = remote(chip_rows, pair_recv, st_s.at[1], st_r.at[1], across)
    slot_rows = pl.ds(pl.multiple_of((group * X + x) * SUMS, SUMS), SUMS)
    slot = table.at[:, :, slot_rows, :]
    x_copies = [remote(slot, slot, x_s.at[n], x_r.at[n], to) for n, to in enumerate(along)]
    side = table.at[:, :, pl.ds(pl.multiple_of(group * X * SUMS, X * SUMS), X * SUMS), :]
    side_copy = remote(side, side, st_s.at[2], st_r.at[2], beside)
    table_copy = remote(table, table, st_s.at[3], st_r.at[3], peer)
    kf_copy = remote(k_hbm.at[:, KEPT * HD : HEADS * HD], kf.at[core], f_s.at[0], f_r.at[0], partner)
    vf_copy = remote(vt.at[KEPT], vf.at[core], f_s.at[1], f_r.at[1], partner)
    kf_pass = remote(kf.at[core], kf.at[core], f_s.at[2], f_r.at[2], peer)
    vf_pass = remote(vf.at[core], vf.at[core], f_s.at[3], f_r.at[3], peer)

    @pl.when(second)
    def _():
        q_copy(0).start()

    @pl.when(first)
    def _():
        kf_copy.start()

    @pl.when(gives)
    def _():
        kx_copy.start()

    def send_queries(h, _):
        q_copy(h).start()
        return 0

    @pl.when(second & leaf)
    def _():
        lax.fori_loop(1, KEPT, send_queries, 0)

    loads[0].wait()
    loads[1].wait()

    offset = lax.broadcasted_iota(jnp.int32, (SUMS, ROWS), 1) + place * ROWS
    row = lax.broadcasted_iota(jnp.int32, (SUMS, ROWS), 0)
    wanted = jnp.zeros((SUMS, ROWS), jnp.int32)
    for c in range(SUMS):
        wanted = jnp.where(row == c, pos_ref[stride, c], wanted)
    pick = jnp.where(offset == wanted, 1.0, 0.0).astype(jnp.bfloat16)

    for part, rows in enumerate((k, v)):
        picked = jnp.dot(pick, rows[...], preferred_element_type=jnp.float32).astype(jnp.bfloat16)
        for h in range(HEADS):
            own_rows[part, h] = picked[:, h * HD : (h + 1) * HD]

    @pl.when(leaf)
    def _():
        rows_copy.start()

    def turn(i, _):
        h = (i + KEPT) % HEADS
        vt[h] = v[:, cols(h)].T

        @pl.when(first & (i == 0))
        def _():
            vf_copy.start()

        @pl.when(gives)
        def _():
            vt_copy(h).start()

        return 0

    lax.fori_loop(0, HEADS, turn, 0)

    @pl.when(hub)
    def _():
        rows_copy.wait_recv()
        chip_rows[...] = own_rows[...] + rows_recv[...]
        pair_copy.start()

    @pl.when(second & hub)
    def _():
        lax.fori_loop(1, KEPT, send_queries, 0)

    loads[2].wait()

    def local(h):
        return attend_causal(k[:, cols(h)], vt[h], q[:, cols(h)])

    def before(h):
        return attend(kx[:, cols(h)], vtx[h], q[:, cols(h)])

    def keep(h, part):
        acc[h], acc_max[h], acc_sum[h] = part

    def kept(h):
        return acc[h], acc_max[h], acc_sum[h]

    column = lax.broadcasted_iota(jnp.int32, (STRIDES * SUMS, 1), 0) // SUMS
    seen = (column % X) * 2 + column // X < stride

    def with_summary(h):
        return join(kept(h), attend(table[0, h], table[1, h].T, q[:, cols(h)], seen))

    def put_out(h, total, weight):
        staged[h] = (total * (1.0 / weight)).astype(jnp.bfloat16).T
        out_copy(h).start()

    def to_x():
        pair_copy.wait_recv()
        table[:, :, slot_rows, :] = chip_rows[...] + pair_recv[...]
        pl.semaphore_wait(barrier, 4)
        for copy in x_copies:
            copy.start()

    def to_side():
        for copy in x_copies:
            copy.wait_recv()
        side_copy.start()

    def to_peer():
        side_copy.wait_recv()
        table_copy.start()

    def wait_peer(h):
        @pl.when(h == 0)
        def _():
            kx_copy.wait_recv()

        vt_copy(h).wait_recv()

    def serve(h):
        queries = qr[h]
        near, far = scores(k[:, cols(h)], queries), scores(kx[:, cols(h)], queries)
        top = jnp.maximum(jnp.max(near, axis=0, keepdims=True), jnp.max(far, axis=0, keepdims=True)) * RATE
        p, p2 = jnp.exp2(near * RATE - top), jnp.exp2(far * RATE - top)
        weight = jnp.sum(p, axis=0, keepdims=True) + jnp.sum(p2, axis=0, keepdims=True)
        total = mix(vt[h], p.astype(jnp.bfloat16)) + mix(vtx[h], p2.astype(jnp.bfloat16))
        o_send[h] = (total * (1.0 / weight)).astype(jnp.bfloat16)
        lse_send[h] = top + jnp.log2(weight)

    def reply(h):
        lse_copy(h).start()
        o_copy(h).start()

    def close(h):
        total, _, weight = with_summary(h)
        put_out(h, total, weight)

    @pl.when(first & hub)
    def _():
        def step(h, _):
            wait_peer(h)
            keep(h, local(h))

            @pl.when(h == 3)
            def _():
                vt_copy(KEPT).wait_recv()
                keep(KEPT, local(KEPT))

            @pl.when(h == 5)
            def _():
                to_peer()

            q_copy(h).wait_recv()
            serve(h)
            reply(h)
            pl.when(h == 1)(to_x)
            pl.when(h == 3)(to_side)
            return 0

        lax.fori_loop(0, KEPT, step, 0)

    @pl.when(first & leaf)
    def _():
        def step(h, _):
            @pl.when(h == 4)
            def _():
                vt_copy(KEPT).wait_recv()
                keep(KEPT, join(local(KEPT), before(KEPT)))

            wait_peer(h)
            keep(h, join(local(h), before(h)))

            q_copy(h).wait_recv()
            serve(h)
            reply(h)
            return 0

        lax.fori_loop(0, KEPT, step, 0)
        table_copy.wait_recv()

    def pass_on(i):
        @pl.when(i == 1)
        def _():
            kf_copy.wait_recv()
            vf_copy.wait_recv()
            kf_pass.start()
            vf_pass.start()

    @pl.when(second & leaf)
    def _():
        def step(i, _):
            h = 2 * i
            keep(h, local(h))
            keep(h + 1, local(h + 1))
            pass_on(i)
            return 0

        lax.fori_loop(0, HEADS // 2, step, 0)

    @pl.when(second & hub)
    def _():
        def step(i, _):
            h = 2 * i
            wait_peer(h)
            vt_copy(h + 1).wait_recv()
            keep(h, join(local(h), before(h)))
            keep(h + 1, join(local(h + 1), before(h + 1)))
            pl.when(i == 1)(to_x)
            pass_on(i)
            pl.when(i == 3)(to_side)
            return 0

        lax.fori_loop(0, HEADS // 2, step, 0)

    @pl.when(first)
    def _():
        def closes(i, _):
            for n in range(4):
                close(4 * i + n)
            return 0

        lax.fori_loop(0, HEADS // 4, closes, 0)

    @pl.when(second)
    def _():
        kf_pass.wait_recv()
        vf_pass.wait_recv()
        queries = q[:, KEPT * HD : HEADS * HD]
        far = join(attend(kf[0], vf[0], queries), attend(kf[1], vf[1], queries))
        keep(KEPT, join(kept(KEPT), far))
        pl.when(hub)(to_peer)

        @pl.when(leaf)
        def _():
            table_copy.wait_recv()

        close(KEPT)

        def finish(h, _):
            keep(h, with_summary(h))
            lse_copy(h).wait_recv()
            o_copy(h).wait_recv()
            total, _, weight = join(kept(h), (o_recv[h].astype(jnp.float32), lse_recv[h], 1.0))
            put_out(h, total, weight)
            return 0

        lax.fori_loop(0, KEPT, finish, 0)

    def drain(h, _):
        out_copy(h).wait()

        @pl.when(gives)
        def _():
            vt_copy(h).wait_send()

        @pl.when(first & (h < KEPT))
        def _():
            o_copy(h).wait_send()
            lse_copy(h).wait_send()

        @pl.when(second & (h < KEPT))
        def _():
            q_copy(h).wait_send()

        return 0

    lax.fori_loop(0, HEADS, drain, 0)

    @pl.when(gives)
    def _():
        kx_copy.wait_send()

    @pl.when(first)
    def _():
        kf_copy.wait_send()
        vf_copy.wait_send()

    @pl.when(second)
    def _():
        kf_pass.wait_send()
        vf_pass.wait_send()

    @pl.when(leaf)
    def _():
        rows_copy.wait_send()

    @pl.when(hub)
    def _():
        for copy in (pair_copy, *x_copies, side_copy, table_copy):
            copy.wait_send()


def on_device(query_rows, key_rows, value_rows, summary_pos):
    bf16, f32 = jnp.bfloat16, jnp.float32
    dma = pltpu.SemaphoreType.DMA
    anywhere = pl.BlockSpec(memory_space=pl.ANY)
    per_head = dma((HEADS,))
    return pl.pallas_call(
        kernel,
        out_shape=jax.ShapeDtypeStruct(query_rows.shape, bf16),
        in_specs=[anywhere] * 3 + [pl.BlockSpec(memory_space=pltpu.SMEM)],
        out_specs=anywhere,
        scratch_shapes=[
            pltpu.VMEM((ROWS, HEADS * HD), bf16),
            pltpu.VMEM((ROWS, HEADS * HD), bf16),
            pltpu.VMEM((ROWS, HEADS * HD), bf16),
            pltpu.VMEM((ROWS, HEADS * HD), bf16),
            pltpu.VMEM((HEADS, HD, ROWS), bf16),
            pltpu.VMEM((HEADS, HD, ROWS), bf16),
            pltpu.VMEM((HEADS, ROWS, HD), bf16),
            pltpu.VMEM((HEADS, HD, ROWS), bf16),
            pltpu.VMEM((HEADS, HD, ROWS), bf16),
            pltpu.VMEM((HEADS, 1, ROWS), f32),
            pltpu.VMEM((HEADS, 1, ROWS), f32),
            pltpu.VMEM((HEADS, HD, ROWS), f32),
            pltpu.VMEM((HEADS, 1, ROWS), f32),
            pltpu.VMEM((HEADS, 1, ROWS), f32),
            pltpu.VMEM((HEADS, ROWS, HD), bf16),
            pltpu.VMEM((2, HEADS, SUMS, HD), bf16),
            pltpu.VMEM((2, HEADS, SUMS, HD), bf16),
            pltpu.VMEM((2, HEADS, SUMS, HD), bf16),
            pltpu.VMEM((2, HEADS, SUMS, HD), bf16),
            pltpu.VMEM((2, HEADS, STRIDES * SUMS, HD), bf16),
            pltpu.VMEM((2, ROWS, HD), bf16),
            pltpu.VMEM((2, HD, ROWS), bf16),
            dma((3,)),
            per_head, per_head,
            dma, dma,
            per_head, per_head,
            per_head, per_head,
            per_head, per_head,
            per_head,
            dma((4,)), dma((4,)),
            dma((X - 1,)), dma((X - 1,)),
            dma((4,)), dma((4,)),
            pltpu.SemaphoreType.REGULAR,
        ],
        compiler_params=pltpu.CompilerParams(
            collective_id=0, has_side_effects=True, vmem_limit_bytes=52 * 2**20
        ),
    )(*(pltpu.with_memory_space_constraint(a, pltpu.HBM) for a in (query_rows, key_rows, value_rows, summary_pos)))


def solution(mesh):
    tokens = P(("dp", "ctx"), None)
    return jax.shard_map(
        on_device,
        mesh=mesh,
        in_specs=(tokens, tokens, tokens, P("dp", None)),
        out_specs=tokens,
        check_vma=False,
    )
```
